32 devices in a mesh: gx: 4 (over y, x), gy: 2 (over core), gz: 4 (over z).
Axes of the slice: x: 2, y: 2, z: 4, core: 2. Of those that a mesh axis runs over, the one named last changes fastest.
Arguments:
- inputs: bfloat16 [4, 32, 32, 256], P(None, 'gx', 'gz', 'gy'), may hold values from -6 to 6
- w_in: bfloat16 [16, 4, 3, 3, 3], replicated, may hold values from -0.875 to 0.875
- w_fine_enc: bfloat16 [16, 16, 3, 3, 3], replicated, may hold values from -0.4375 to 0.4375
- w_down_mid: bfloat16 [64, 16, 2, 2, 2], replicated, may hold values from -0.75 to 0.75
- w_mid_enc: bfloat16 [27, 4096], replicated, may hold values from -0.21875 to 0.21875
- w_down_bottom: bfloat16 [8, 16384], replicated, may hold values from -0.375 to 0.375
- w_query: bfloat16 [256, 256], replicated, may hold values from -8 to 8
- w_key: bfloat16 [256, 256], replicated, may hold values from -0.375 to 0.375
- w_value: bfloat16 [256, 256], replicated, may hold values from -0.375 to 0.375
- w_attn_out: bfloat16 [256, 256], replicated, may hold values from -0.375 to 0.375
- w_up_mid: bfloat16 [8, 16384], replicated, may hold values from -0.375 to 0.375
- w_mid_dec: bfloat16 [27, 4096], replicated, may hold values from -0.21875 to 0.21875
- w_up_fine: bfloat16 [64, 16, 2, 2, 2], replicated, may hold values from -0.75 to 0.75
- w_fine_dec: bfloat16 [16, 16, 3, 3, 3], replicated, may hold values from -0.4375 to 0.4375
- w_head: bfloat16 [4, 16], replicated, may hold values from -1.5 to 1.5
Outputs:
- wake: float32 [4, 32, 32, 256], P(None, 'gx', 'gz', 'gy')
The draws below stay inside these ranges and needn't reach their ends.
All inputs are finite; a program needn't handle non-finite values.
Results may differ from the reference program's by a relative error of at most 0.023.
The reference program's roundings to bfloat16 on the way count: a program that leaves them out, or rounds other values in their place, can miss the bound.
Values may be sent and summed in bfloat16 or wider, within the bound.
A program may use at most 64 MiB of HBM per device.

```python
import jax
import jax.numpy as jnp
from jax import lax

CH_IN = 4
C0 = 16
C1 = 64
C2 = 256
HEADS = 4
HEAD_DIM = 64
CH_OUT = 4
NX = 32
NV = 32
NS = 256


def draw_w_query(key, part):
    first_key = jax.random.fold_in(key, 11)
    base = jax.random.normal(first_key, (C2, C2), jnp.float32) * C2 ** (-0.5)
    return jnp.clip(base, -8.0, 8.0).astype(jnp.bfloat16)


def shard_levels(stream_key, extent, split, low, largest):
    loudness = 1.0
    for dim, parts in split:
        heights = jax.random.uniform(jax.random.fold_in(jax.random.fold_in(stream_key, 6), dim), (parts,), jnp.float32, low / len(split), largest / len(split))
        loudness = loudness * jnp.repeat(jnp.exp(heights), extent[dim] // parts).reshape((-1,) + (1,) * (len(extent) - 1 - dim))
    return loudness


def scatter_about(stream_key, shape, deviation, bound, split=(), kind=jnp.bfloat16):
    values = jax.random.normal(stream_key, shape, jnp.float32) * deviation
    if len(split) > 0:
        values = shard_levels(stream_key, shape, split, -0.22, 0.18) * values
    return jnp.clip(values, min=-bound, max=bound).astype(kind)


def setup_inputs(seed: int = 0) -> dict:
    arg_keys = jax.random.split(jax.random.key(seed), 16)
    inputs = scatter_about(arg_keys[0], (CH_IN, NX, NV, NS), 1.0, 6.0, ((1, 4), (2, 4), (3, 2)))
    w_in = scatter_about(arg_keys[1], (C0, CH_IN, 3, 3, 3), (CH_IN * 27 // 2) ** -0.5, 0.875)
    w_fine_enc = scatter_about(arg_keys[2], (C0, C0, 3, 3, 3), (C0 * 27 // 2) ** -0.5, 0.4375)
    w_down_mid = scatter_about(arg_keys[3], (C1, C0, 2, 2, 2), (C0 * 4) ** -0.5, 0.75)
    w_mid_enc = scatter_about(arg_keys[4], (27, C1 * C1), (C1 * 27 // 2) ** -0.5, 0.21875)
    w_down_bottom = scatter_about(arg_keys[5], (8, C2 * C1), (C1 * 4) ** -0.5, 0.375)
    w_query = draw_w_query(jax.random.fold_in(arg_keys[15], 71), 0)
    w_key = scatter_about(arg_keys[7], (C2, C2), C2 ** -0.5, 0.375)
    w_value = scatter_about(arg_keys[8], (C2, C2), C2 ** -0.5, 0.375)
    w_attn_out = scatter_about(arg_keys[9], (C2, C2), C2 ** -0.5, 0.375)
    w_up_mid = scatter_about(arg_keys[10], (8, C2 * C1), C2 ** -0.5, 0.375)
    w_mid_dec = scatter_about(arg_keys[11], (27, C1 * C1), (C1 * 27 // 2) ** -0.5, 0.21875)
    w_up_fine = scatter_about(arg_keys[12], (C1, C0, 2, 2, 2), C1 ** -0.5, 0.75)
    w_fine_dec = scatter_about(arg_keys[13], (C0, C0, 3, 3, 3), (C0 * 27 // 2) ** -0.5, 0.4375)
    w_head = scatter_about(arg_keys[14], (CH_OUT, C0), C0 ** -0.5, 1.5)
    return dict(inputs=inputs, w_in=w_in, w_fine_enc=w_fine_enc, w_down_mid=w_down_mid, w_mid_enc=w_mid_enc, w_down_bottom=w_down_bottom, w_query=w_query, w_key=w_key, w_value=w_value, w_attn_out=w_attn_out, w_up_mid=w_up_mid, w_mid_dec=w_mid_dec, w_up_fine=w_up_fine, w_fine_dec=w_fine_dec, w_head=w_head)


HIGH = lax.Precision.HIGHEST
NUMS = ('NCDHW', 'OIDHW', 'NCDHW')

def unfold(weight, side, first, second):
    return weight.reshape(side, side, side, first, second).transpose(3, 4, 0, 1, 2)

def conv_same(field, weight):
    padded = jnp.pad(field.astype(jnp.float32), ((0, 0), (1, 1), (1, 1), (1, 1)))
    return lax.conv_general_dilated(padded[None], weight.astype(jnp.float32), (1, 1, 1), 'VALID', dimension_numbers=NUMS, precision=HIGH)[0]

def conv_down(field, weight):
    return lax.conv_general_dilated(field.astype(jnp.float32)[None], weight.astype(jnp.float32), (2, 2, 2), 'VALID', dimension_numbers=NUMS, precision=HIGH)[0]

def conv_up(field, weight):
    outer = jnp.einsum('ixvs,ioabc->oxavbsc', field.astype(jnp.float32), weight.astype(jnp.float32), precision=HIGH)
    chans, sx, sv, ss = (weight.shape[1], field.shape[1], field.shape[2], field.shape[3])
    return outer.reshape(chans, 2 * sx, 2 * sv, 2 * ss)

def activate(value):
    return jax.nn.silu(value).astype(jnp.bfloat16)

def project(weight, field):
    return jnp.einsum('oc,cxp->oxp', weight.astype(jnp.float32), field.astype(jnp.float32), precision=HIGH)

def reference(inputs, w_in, w_fine_enc, w_down_mid, w_mid_enc, w_down_bottom, w_query, w_key, w_value, w_attn_out, w_up_mid, w_mid_dec, w_up_fine, w_fine_dec, w_head):
    first = activate(conv_same(inputs, w_in))
    fine_skip = activate(conv_same(first, w_fine_enc))
    mid_in = activate(conv_down(fine_skip, w_down_mid))
    mid_skip = activate(conv_same(mid_in, unfold(w_mid_enc, 3, C1, C1)))
    bottom = activate(conv_down(mid_skip, unfold(w_down_bottom, 2, C2, C1)))
    chans, sx, sv, ss = bottom.shape
    flat = bottom.reshape(chans, sx, sv * ss)
    values_f = flat.astype(jnp.float32)
    mean_sq = lax.optimization_barrier(jnp.mean(values_f * values_f, axis=0))
    normed = (values_f * lax.rsqrt(mean_sq + 1e-05)).astype(jnp.bfloat16)
    queries = project(w_query, normed).astype(jnp.bfloat16).reshape(HEADS, HEAD_DIM, sx, sv * ss)
    keys = project(w_key, normed).astype(jnp.bfloat16).reshape(HEADS, HEAD_DIM, sx, sv * ss)
    values = project(w_value, normed).astype(jnp.bfloat16).reshape(HEADS, HEAD_DIM, sx, sv * ss)
    scores = jnp.einsum('hdxp,hdyp->hxyp', queries.astype(jnp.float32), keys.astype(jnp.float32), precision=HIGH) / jnp.sqrt(jnp.float32(HEAD_DIM))
    weights = jax.nn.softmax(scores, axis=2).astype(jnp.bfloat16)
    attended = jnp.einsum('hxyp,hdyp->hdxp', weights.astype(jnp.float32), values.astype(jnp.float32), precision=HIGH)
    attended = attended.astype(jnp.bfloat16).reshape(chans, sx, sv * ss)
    bottom_out = (values_f + project(w_attn_out, attended)).astype(jnp.bfloat16).reshape(chans, sx, sv, ss)
    mid_up = (conv_up(bottom_out, unfold(w_up_mid, 2, C2, C1)) + mid_skip.astype(jnp.float32)).astype(jnp.bfloat16)
    mid_dec = activate(conv_same(mid_up, unfold(w_mid_dec, 3, C1, C1)))
    fine_up = (conv_up(mid_dec, w_up_fine) + fine_skip.astype(jnp.float32)).astype(jnp.bfloat16)
    fine_dec = activate(conv_same(fine_up, w_fine_dec))
    return jnp.einsum('oc,cxvs->oxvs', w_head.astype(jnp.float32), fine_dec.astype(jnp.float32), precision=HIGH)
```

```python
import functools

import jax
import jax.numpy as jnp
import numpy as np
from jax import lax
from jax.experimental import pallas as pl
from jax.experimental.pallas import tpu as pltpu
from jax.sharding import PartitionSpec as P

BF = jnp.bfloat16
F32 = jnp.float32
MESH = pl.DeviceIdType.MESH
HEADS = 4
DIRS = tuple((dx, dv) for dx in (-1, 0, 1) for dv in (-1, 0, 1) if (dx, dv) != (0, 0))


def constants(nx, nv, ns):
    mv, ms, bv, bs = nv // 2, ns // 2, nv // 4, ns // 4
    g_first = np.zeros((nv + 2, 3, 3, 4, 3, nv + 8, 4), np.float32)
    for k in range(nv + 2):
        for a in range(3):
            for b in range(3):
                for i in range(4):
                    g_first[k, a, b, i, a, k + b + 2, i] = 1
    g_fine = np.zeros((nv, 3, 3, 16, 3, nv + 2, 16), np.float32)
    for k in range(nv):
        for a in range(3):
            for b in range(3):
                for i in range(16):
                    g_fine[k, a, b, i, a, k + b, i] = 1
    g_down = np.zeros((mv, 2, 2, 16, 2, nv, 16), np.float32)
    for k in range(mv):
        for a in range(2):
            for b in range(2):
                for i in range(16):
                    g_down[k, a, b, i, a, 2 * k + b, i] = 1
    g_up = np.zeros((mv, 2, 64, 2, mv, 64), np.float32)
    for k in range(mv):
        for c in range(2):
            for i in range(64):
                g_up[k, c, i, c, k, i] = 1
    lane_down = np.zeros((ns, 2, 2, ms), np.float32)
    for c in range(2):
        for t in range(ms):
            lane_down[2 * t + c, c, :, t] = 1
    cells = 2 * bv * bs
    lane_bottom = np.zeros((2 * bv, ns, 2, 2 * bv, bs), np.float32)
    for q in range(2 * bv):
        for c in range(2):
            for t in range(bs):
                lane_bottom[q, 2 * t + c, c, q, t] = 1
    lane_mid = np.zeros((2 * bv, bs, 2 * bv, 2, 2, ms), np.float32)
    for q in range(2 * bv):
        for c in range(2):
            for t in range(bs):
                lane_mid[q, t, q, c, :, 2 * t + c] = 1
    lane_fine = np.zeros((ns, 2, ns), np.float32)
    for c in range(2):
        for u in range(ms):
            lane_fine[u, c, 2 * u + c] = 1
    arrays = (
        g_first.reshape(nv + 2, 36, 3 * (nv + 8) * 4),
        g_fine.reshape(nv, 144, 3 * (nv + 2) * 16),
        g_down.reshape(mv, 64, 2 * nv * 16),
        g_up.reshape(mv, 128, 2 * mv * 64),
        lane_down.reshape(ns, 2 * ns),
        lane_bottom.reshape(2 * bv, ns, 2 * cells),
        lane_mid.reshape(cells, 2 * bv * 2 * ns),
        lane_fine.reshape(ns, 2 * ns),
    )
    return tuple(jnp.asarray(np.asarray(a, jnp.bfloat16)) for a in arrays)


def dot(a, b):
    return jnp.dot(a, b, preferred_element_type=F32)


def silu(x):
    h = 0.5 * x
    return h + h * jnp.tanh(h)


def rows(ref, x, n):
    part = ref[pl.ds(x, n)]
    return part.reshape(n * part.shape[1], part.shape[2])


def taps(z, m):
    n = z.shape[1]
    return pltpu.roll(z[0:m], 1, 1) + z[m : 2 * m] + pltpu.roll(z[2 * m : 3 * m], n - 1, 1)


def kernel(
    gx, gz, nx, nv, ns,
    inp, w_first, w_enc, w_down, w_menc, w_bot, w_q, w_k, w_v, w_o, w_umid, w_mdec, w_ufine, w_dec, w_hd,
    g_first, g_fine, g_down, g_up, l_down, l_bottom, l_mid, l_fine,
    out,
    p_in, q_in, p_mi, q_mi, p_mu, q_mu, p_fu, q_fu,
    t_first, t_enc, t_dec, t_down, t_up, first, skip, mskip, mdec, bottom, gathered,
    send, recv, csend, crecv, asend, arecv,
):
    mx, mv = nx // 2, nv // 2
    bx, bv = nx // 4, nv // 4
    ix, iy, iz = lax.axis_index("gx"), lax.axis_index("gy"), lax.axis_index("gz")

    def inside(dx, dv):
        ok = None
        for d, i, n in ((dx, ix, gx), (dv, iz, gz)):
            if d:
                here = (i + d >= 0) & (i + d < n)
                ok = here if ok is None else ok & here
        return ok

    def target(dx, dv):
        return (ix + dx, iy, iz + dv)

    for ref in (p_in, p_mi, p_mu, p_fu):
        ref[...] = jnp.zeros_like(ref)

    barrier = pltpu.get_barrier_semaphore()
    pl.semaphore_signal(barrier, inc=1, device_id=(ix, 1 - iy, iz), device_id_type=MESH)
    for d in range(1, gx):
        pl.semaphore_signal(
            barrier, inc=1, device_id=(lax.rem(ix + d, gx), iy, iz), device_id_type=MESH
        )
    count = gx
    for dx, dv in DIRS:
        if dv:
            ok = inside(dx, dv)

            @pl.when(ok)
            def _(dx=dx, dv=dv):
                pl.semaphore_signal(barrier, inc=1, device_id=target(dx, dv), device_id_type=MESH)

            count = count + ok.astype(jnp.int32)
    pl.semaphore_wait(barrier, count)

    def span(d, width, size, unit):
        if d > 0:
            return pl.ds(size * unit, width * unit), pl.ds(0, width * unit)
        if d < 0:
            return pl.ds(width * unit, width * unit), pl.ds((width + size) * unit, width * unit)
        return pl.ds(width * unit, size * unit), pl.ds(width * unit, size * unit)

    def copies(e, p, wx, sx, wv, sv, unit):
        made = []
        for n, (dx, dv) in enumerate(DIRS):
            src_x, dst_x = span(dx, wx, sx, 1)
            src_v, dst_v = span(dv, wv, sv, unit)
            made.append(
                pltpu.make_async_remote_copy(
                    src_ref=p.at[src_x, src_v],
                    dst_ref=p.at[dst_x, dst_v],
                    send_sem=send.at[e, n],
                    recv_sem=recv.at[e, n],
                    device_id=target(dx, dv),
                    device_id_type=MESH,
                )
            )
        return made

    def begin(made):
        for c, (dx, dv) in zip(made, DIRS):
            pl.when(inside(dx, dv))(c.start)

    def finish(e, made, p, q):
        for c, (dx, dv) in zip(made, DIRS):
            pl.when(inside(-dx, -dv))(c.wait_recv)
        across = pltpu.make_async_remote_copy(
            src_ref=p, dst_ref=q, send_sem=csend.at[e], recv_sem=crecv.at[e],
            device_id=(ix, 1 - iy, iz), device_id_type=MESH,
        )
        across.start()
        for c, (dx, dv) in zip(made, DIRS):
            pl.when(inside(dx, dv))(c.wait_send)
        return across

    lane = lax.broadcasted_iota(jnp.int32, (1, ns), 1)

    def edge(width):
        low = jnp.where(iy == 0, 0, ns - width)
        return jnp.where((lane >= low) & (lane < low + width), 1.0, 0.0).astype(BF)

    unit = inp.shape[1] // nv
    p_in[2 : 2 + nx, 4 * unit : (4 + nv) * unit] = inp[...]
    made = copies(0, p_in, 2, nx, 4, nv, unit)
    begin(made)
    for k in range(nv + 2):
        part = dot(w_first[...], g_first[k]).astype(BF)
        for c in range(3):
            t_first[(c * (nv + 2) + k) * 16 : (c * (nv + 2) + k + 1) * 16] = part[c * 16 : c * 16 + 16]
    across = finish(0, made, p_in, q_in)
    for src, dst in ((w_enc, t_enc), (w_dec, t_dec)):
        for k in range(nv):
            part = dot(src[...], g_fine[k]).astype(BF)
            for c in range(3):
                dst[(c * nv + k) * 16 : (c * nv + k + 1) * 16] = part[c * 16 : c * 16 + 16]
    across.wait()

    e2, e1 = edge(2), edge(1)
    fine_rows = (nv + 2) * 16
    row = lax.broadcasted_iota(jnp.int32, (fine_rows, 1), 0)
    v_low = jnp.where(iz > 0, 0, 16)
    v_high = jnp.where(iz < gz - 1, fine_rows, fine_rows - 16)
    v_ok = jnp.where((row >= v_low) & (row < v_high), 1.0, 0.0)
    both = jnp.concatenate([jnp.ones((1, ns), F32), e1.astype(F32)], axis=1)
    keep_first = v_ok * both

    def first_step(x, _):
        field = jnp.concatenate([rows(p_in, x, 3), rows(q_in, x, 3) * e2], axis=1)
        z = taps(dot(t_first[...], field), fine_rows)
        gone = ((x == 0) & (ix == 0)) | ((x == nx + 1) & (ix == gx - 1))
        first[x] = (silu(z) * keep_first * jnp.where(gone, 0.0, 1.0)).astype(BF)
        return 0

    lax.fori_loop(0, nx + 2, first_step, 0)

    def enc_step(x, _):
        z = taps(dot(t_enc[...], rows(first, x, 3)), nv * 16)[:, :ns]
        skip[x] = silu(z).astype(BF)
        return 0

    lax.fori_loop(0, nx, enc_step, 0)

    for k in range(mv):
        part = dot(w_down[...], g_down[k]).astype(BF)
        half = g_down.shape[2]
        for c in range(2):
            t_down[k * 64 : (k + 1) * 64, c * half : (c + 1) * half] = part[c * 64 : (c + 1) * 64]

    def down_step(x, _):
        y = dot(rows(skip, 2 * x, 2), l_down[...]).astype(BF)
        field = jnp.concatenate([y[:, :ns], y[:, ns:]], axis=0)
        p_mi[x + 1, 64 : (mv + 1) * 64] = silu(dot(t_down[...], field)).astype(BF)
        return 0

    lax.fori_loop(0, mx, down_step, 0)

    made = copies(1, p_mi, 1, mx, 1, mv, 64)
    begin(made)
    for k in range(mv):
        part = dot(w_ufine[...], g_up[k]).astype(BF)
        for a in range(2):
            t_up[a * nv * 16 + k * 32 : a * nv * 16 + k * 32 + 32] = part[a * 32 : a * 32 + 32]
    finish(1, made, p_mi, q_mi).wait()

    own_half = jnp.where(lane < ns // 2, 1.0, 0.0).astype(BF)
    mid_edge = jnp.where(lane == jnp.where(iy == 0, ns // 2, ns - 1), 1.0, 0.0).astype(BF)

    def mid_conv(w, p, q, x, v):
        pieces = []
        for a in range(3):
            r = pl.ds(pl.multiple_of(v * 64, 64), 192)
            pieces.append(p[x + a, r] * own_half + q[x + a, r] * mid_edge)
        z = silu(taps(dot(w[...], jnp.concatenate(pieces, axis=0)), 64))
        return jnp.where(lane < ns // 2, z, pltpu.roll(z, ns // 2, 1)).astype(BF)

    def menc_step(n, _):
        x, v = n // mv, n % mv
        mskip[x, pl.ds(pl.multiple_of(v * 64, 64), 64)] = mid_conv(w_menc, p_mi, q_mi, x, v)
        return 0

    lax.fori_loop(0, mx * mv, menc_step, 0)

    halves = []
    for a in range(2):
        total = None
        for n in range(bx * bv):
            x, v = n // bv, n % bv
            term = dot(mskip[2 * x + a, v * 128 : v * 128 + 128], l_bottom[n])
            total = term if total is None else total + term
        halves.append(total.astype(BF))
    field = jnp.concatenate(
        [halves[0][:, :ns], halves[1][:, :ns], halves[0][:, ns:], halves[1][:, ns:]], axis=0
    )
    bottom[...] = silu(dot(w_bot[...], field)).astype(BF)

    peers = []
    for d in range(1, gx):
        c = pltpu.make_async_remote_copy(
            src_ref=bottom, dst_ref=gathered.at[d - 1], send_sem=asend.at[d - 1], recv_sem=arecv.at[d - 1],
            device_id=(lax.rem(ix + d, gx), iy, iz), device_id_type=MESH,
        )
        c.start()
        peers.append(c)

    def normalize(block):
        f = block.astype(F32)
        return (f * lax.rsqrt(jnp.mean(f * f, axis=0, keepdims=True) + 1e-05)).astype(BF)

    chans = bottom.shape[0]
    depth = chans // HEADS
    own = normalize(bottom[...])
    queries = dot(w_q[...], own).astype(BF).astype(F32)
    scores, values = [], []
    for d in range(gx):
        if d:
            peers[d - 1].wait()
            normed = normalize(gathered[d - 1])
        else:
            normed = own
        keys = dot(w_k[...], normed).astype(BF).astype(F32)
        value = dot(w_v[...], normed).astype(BF).astype(F32)
        for turn in range(bx):
            k = pltpu.roll(keys, turn * (ns // bx), 1) if turn else keys
            v = pltpu.roll(value, turn * (ns // bx), 1) if turn else value
            scores.append(
                jnp.sum((queries * k).reshape(HEADS, depth, ns), axis=1, keepdims=True) * (depth**-0.5)
            )
            values.append(v)
    top = functools.reduce(jnp.maximum, scores)
    powers = [jnp.exp(s - top) for s in scores]
    norm = 1.0 / functools.reduce(jnp.add, powers)
    attended = None
    for s, v in zip(powers, values):
        term = (s * norm).astype(BF).astype(F32) * v.reshape(HEADS, depth, ns)
        attended = term if attended is None else attended + term
    attended = attended.reshape(chans, ns).astype(BF)
    mixed = (bottom[...].astype(F32) + dot(w_o[...], attended)).astype(BF)

    spread = dot(mixed, l_mid[...]).astype(BF)
    for n in range(bx * bv):
        x, v = n // bv, n % bv
        field = jnp.concatenate(
            [spread[:, 2 * n * ns : (2 * n + 1) * ns], spread[:, (2 * n + 1) * ns : (2 * n + 2) * ns]], axis=0
        )
        z = dot(w_umid[...], field)
        for a in range(2):
            old = mskip[2 * x + a, v * 128 : v * 128 + 128].astype(F32)
            p_mu[2 * x + a + 1, 64 + v * 128 : 64 + v * 128 + 128] = (z[a * 128 : a * 128 + 128] + old).astype(BF)

    made = copies(2, p_mu, 1, mx, 1, mv, 64)
    begin(made)
    finish(2, made, p_mu, q_mu).wait()

    def mdec_step(n, _):
        x, v = n // mv, n % mv
        mdec[x, pl.ds(pl.multiple_of(v * 64, 64), 64)] = mid_conv(w_mdec, p_mu, q_mu, x, v)
        return 0

    lax.fori_loop(0, mx * mv, mdec_step, 0)

    def up_step(x, _):
        y = dot(mdec[x], l_fine[...]).astype(BF)
        field = jnp.concatenate([y[:, :ns], y[:, ns:]], axis=0)
        z = dot(t_up[...], field)
        m = nv * 16
        for a in range(2):
            old = skip[2 * x + a].astype(F32)
            p_fu[2 * x + a + 1, 16 : 16 + m] = (z[a * m : (a + 1) * m] + old).astype(BF)
        return 0

    lax.fori_loop(0, mx, up_step, 0)

    made = copies(3, p_fu, 1, nx, 1, nv, 16)
    begin(made)
    finish(3, made, p_fu, q_fu).wait()

    def dec_step(x, _):
        field = jnp.concatenate([rows(p_fu, x, 3), rows(q_fu, x, 3) * e1], axis=1)
        z = taps(dot(t_dec[...], field), nv * 16)[:, :ns]
        wake = dot(w_hd[...], silu(z).astype(BF))
        for o in range(4):
            out[o, x] = wake[o * nv : (o + 1) * nv]
        return 0

    lax.fori_loop(0, nx, dec_step, 0)


def on_device(
    gx, gz, inputs, w_in, w_fine_enc, w_down_mid, w_mid_enc, w_down_bottom, w_query, w_key, w_value,
    w_attn_out, w_up_mid, w_mid_dec, w_up_fine, w_fine_dec, w_head,
):
    _, nx, nv, ns = inputs.shape
    mx, mv = nx // 2, nv // 2
    cells = (nx // 4) * (nv // 4) * (ns // 4)
    assert cells == ns and 2 * (nx // 4) == mx

    def taps_out(w):
        o, i = w.shape[:2]
        return w.transpose(4, 0, 2, 3, 1).reshape(w.shape[4] * o, -1)

    def mid(w):
        return w.reshape(3, 3, 3, 64, 64).transpose(2, 3, 0, 1, 4).reshape(192, 576)

    local = inputs.transpose(1, 2, 0, 3).reshape(nx, nv * 4, ns)
    w_bot = w_down_bottom.reshape(2, 2, 2, 256, 64).transpose(3, 2, 0, 1, 4).reshape(256, 512)
    w_umid = w_up_mid.reshape(2, 2, 2, 256, 64).transpose(0, 1, 4, 2, 3).reshape(256, 512)
    w_ufine = w_up_fine.transpose(2, 3, 1, 4, 0).reshape(64, 128)
    w_hd = (w_head[:, None, None, :] * jnp.eye(nv, dtype=BF)[None, :, :, None]).reshape(4 * nv, nv * 16)
    operands = (
        local, taps_out(w_in), taps_out(w_fine_enc), taps_out(w_down_mid), mid(w_mid_enc), w_bot,
        w_query, w_key, w_value, w_attn_out, w_umid, mid(w_mid_dec), w_ufine, taps_out(w_fine_dec), w_hd,
    ) + constants(nx, nv, ns)
    vm = pltpu.VMEM
    shapes = []
    for shape in (
        (nx + 4, (nv + 8) * 4, ns), (mx + 2, (mv + 2) * 64, ns), (mx + 2, (mv + 2) * 64, ns),
        (nx + 2, (nv + 2) * 16, ns),
    ):
        shapes += [vm(shape, BF), vm(shape, BF)]
    return pl.pallas_call(
        functools.partial(kernel, gx, gz, nx, nv, ns),
        out_shape=jax.ShapeDtypeStruct(inputs.shape, F32),
        in_specs=[pl.BlockSpec(memory_space=pltpu.VMEM)] * len(operands),
        out_specs=pl.BlockSpec(memory_space=pltpu.VMEM),
        scratch_shapes=shapes + [
            vm((3 * (nv + 2) * 16, 3 * (nv + 8) * 4), BF),
            vm((3 * nv * 16, 3 * (nv + 2) * 16), BF),
            vm((3 * nv * 16, 3 * (nv + 2) * 16), BF),
            vm((mv * 64, 4 * nv * 16), BF),
            vm((2 * nv * 16, 2 * mv * 64), BF),
            vm((nx + 2, (nv + 2) * 16, 2 * ns), BF),
            vm((nx, nv * 16, ns), BF),
            vm((mx, mv * 64, ns), BF),
            vm((mx, mv * 64, ns), BF),
            vm((256, cells), BF),
            vm((max(gx - 1, 1), 256, cells), BF),
            pltpu.SemaphoreType.DMA((4, 8)),
            pltpu.SemaphoreType.DMA((4, 8)),
            pltpu.SemaphoreType.DMA((4,)),
            pltpu.SemaphoreType.DMA((4,)),
            pltpu.SemaphoreType.DMA((max(gx - 1, 1),)),
            pltpu.SemaphoreType.DMA((max(gx - 1, 1),)),
        ],
        compiler_params=pltpu.CompilerParams(
            collective_id=0, has_side_effects=True, vmem_limit_bytes=48 * 1024 * 1024
        ),
    )(*operands)


def solution(mesh):
    cells = P(None, "gx", "gz", "gy")
    return jax.shard_map(
        functools.partial(on_device, mesh.shape["gx"], mesh.shape["gz"]),
        mesh=mesh, in_specs=(cells,) + (P(),) * 14, out_specs=cells, check_vma=False,
    )
```

```python
import functools

import jax
import jax.numpy as jnp
import numpy as np
from jax import lax
from jax.experimental import pallas as pl
from jax.experimental.pallas import tpu as pltpu
from jax.sharding import PartitionSpec as P

BF = jnp.bfloat16
F32 = jnp.float32
MESH = pl.DeviceIdType.MESH
HEADS = 4
DIRS = tuple((dx, dv) for dx in (-1, 0, 1) for dv in (-1, 0, 1) if (dx, dv) != (0, 0))


def constants(nx, nv, ns):
    mv, ms, bv, bs = nv // 2, ns // 2, nv // 4, ns // 4
    g_first = np.zeros((nv + 2, 3, 3, 4, 3, nv + 8, 4), np.float32)
    for k in range(nv + 2):
        for a in range(3):
            for b in range(3):
                for i in range(4):
                    g_first[k, a, b, i, a, k + b + 2, i] = 1
    g_fine = np.zeros((nv, 3, 3, 16, 3, nv + 2, 16), np.float32)
    for k in range(nv):
        for a in range(3):
            for b in range(3):
                for i in range(16):
                    g_fine[k, a, b, i, a, k + b, i] = 1
    g_down = np.zeros((mv, 2, 2, 16, 2, nv, 16), np.float32)
    for k in range(mv):
        for a in range(2):
            for b in range(2):
                for i in range(16):
                    g_down[k, a, b, i, a, 2 * k + b, i] = 1
    g_up = np.zeros((mv, 2, 64, 2, mv, 64), np.float32)
    for k in range(mv):
        for c in range(2):
            for i in range(64):
                g_up[k, c, i, c, k, i] = 1
    lane_down = np.zeros((ns, 2, 2, ms), np.float32)
    for c in range(2):
        for t in range(ms):
            lane_down[2 * t + c, c, :, t] = 1
    cells = 2 * bv * bs
    lane_bottom = np.zeros((2 * bv, ns, 2, 2 * bv, bs), np.float32)
    for q in range(2 * bv):
        for c in range(2):
            for t in range(bs):
                lane_bottom[q, 2 * t + c, c, q, t] = 1
    lane_mid = np.zeros((2 * bv, bs, 2 * bv, 2, 2, ms), np.float32)
    for q in range(2 * bv):
        for c in range(2):
            for t in range(bs):
                lane_mid[q, t, q, c, :, 2 * t + c] = 1
    lane_fine = np.zeros((ns, 2, ns), np.float32)
    for c in range(2):
        for u in range(ms):
            lane_fine[u, c, 2 * u + c] = 1
    arrays = (
        g_first.reshape(nv + 2, 36, 3 * (nv + 8) * 4),
        g_fine.reshape(nv, 144, 3 * (nv + 2) * 16),
        g_down.reshape(mv, 64, 2 * nv * 16),
        g_up.reshape(mv, 128, 2 * mv * 64),
        lane_down.reshape(ns, 2 * ns),
        lane_bottom.reshape(2 * bv, ns, 2 * cells),
        lane_mid.reshape(cells, 2 * bv * 2 * ns),
        lane_fine.reshape(ns, 2 * ns),
    )
    return tuple(jnp.asarray(np.asarray(a, jnp.bfloat16)) for a in arrays)


def dot(a, b):
    return jnp.dot(a, b, preferred_element_type=F32)


def silu(x):
    h = 0.5 * x
    return h + h * jnp.tanh(h)


def rows(ref, x, n):
    part = ref[pl.ds(x, n)]
    return part.reshape(n * part.shape[1], part.shape[2])


def by_tap(ref):
    parts = []
    for c in range(3):
        parts.append(jnp.concatenate([ref[ab * 3 + c].astype(F32) for ab in range(9)], axis=1))
    return jnp.concatenate(parts, axis=0).astype(BF)


def taps(z, m):
    n = z.shape[1]
    return pltpu.roll(z[0:m], 1, 1) + z[m : 2 * m] + pltpu.roll(z[2 * m : 3 * m], n - 1, 1)


def kernel(
    gx, gz, nx, nv, ns,
    inp, w_first, w_enc, w_down, w_menc, w_bot, w_q, w_k, w_v, w_o, w_umid, w_mdec, w_ufine, w_dec, w_hd,
    g_first, g_fine, g_down, g_up, l_down, l_bottom, l_mid, l_fine,
    out,
    p_in, q_in, p_mi, q_mi, p_mu, q_mu, p_fu, q_fu,
    t_first, t_enc, t_dec, t_down, t_up, first, skip, mskip, mdec, bottom, gathered,
    send, recv, csend, crecv, asend, arecv,
):
    mx, mv = nx // 2, nv // 2
    bx, bv = nx // 4, nv // 4
    ix, iy, iz = lax.axis_index("gx"), lax.axis_index("gy"), lax.axis_index("gz")

    def inside(dx, dv):
        ok = None
        for d, i, n in ((dx, ix, gx), (dv, iz, gz)):
            if d:
                here = (i + d >= 0) & (i + d < n)
                ok = here if ok is None else ok & here
        return ok

    def target(dx, dv):
        return (ix + dx, iy, iz + dv)

    for ref in (p_in, p_mi, p_mu, p_fu):
        ref[...] = jnp.zeros_like(ref)

    barrier = pltpu.get_barrier_semaphore()
    pl.semaphore_signal(barrier, inc=1, device_id=(ix, 1 - iy, iz), device_id_type=MESH)
    for d in range(1, gx):
        pl.semaphore_signal(
            barrier, inc=1, device_id=(lax.rem(ix + d, gx), iy, iz), device_id_type=MESH
        )
    count = gx
    for dx, dv in DIRS:
        if dv:
            ok = inside(dx, dv)

            @pl.when(ok)
            def _(dx=dx, dv=dv):
                pl.semaphore_signal(barrier, inc=1, device_id=target(dx, dv), device_id_type=MESH)

            count = count + ok.astype(jnp.int32)
    pl.semaphore_wait(barrier, count)

    def span(d, width, size, unit):
        if d > 0:
            return pl.ds(size * unit, width * unit), pl.ds(0, width * unit)
        if d < 0:
            return pl.ds(width * unit, width * unit), pl.ds((width + size) * unit, width * unit)
        return pl.ds(width * unit, size * unit), pl.ds(width * unit, size * unit)

    def copies(e, p, wx, sx, wv, sv, unit):
        made = []
        for n, (dx, dv) in enumerate(DIRS):
            src_x, dst_x = span(dx, wx, sx, 1)
            src_v, dst_v = span(dv, wv, sv, unit)
            made.append(
                pltpu.make_async_remote_copy(
                    src_ref=p.at[src_x, src_v],
                    dst_ref=p.at[dst_x, dst_v],
                    send_sem=send.at[e, n],
                    recv_sem=recv.at[e, n],
                    device_id=target(dx, dv),
                    device_id_type=MESH,
                )
            )
        return made

    def begin(made):
        for c, (dx, dv) in zip(made, DIRS):
            pl.when(inside(dx, dv))(c.start)

    def finish(e, made, p, q):
        for c, (dx, dv) in zip(made, DIRS):
            pl.when(inside(-dx, -dv))(c.wait_recv)
        across = pltpu.make_async_remote_copy(
            src_ref=p, dst_ref=q, send_sem=csend.at[e], recv_sem=crecv.at[e],
            device_id=(ix, 1 - iy, iz), device_id_type=MESH,
        )
        across.start()
        for c, (dx, dv) in zip(made, DIRS):
            pl.when(inside(dx, dv))(c.wait_send)
        return across

    lane = lax.broadcasted_iota(jnp.int32, (1, ns), 1)

    def edge(width):
        low = jnp.where(iy == 0, 0, ns - width)
        return jnp.where((lane >= low) & (lane < low + width), 1.0, 0.0).astype(BF)

    unit = inp.shape[1] // nv
    p_in[2 : 2 + nx, 4 * unit : (4 + nv) * unit] = inp[...]
    made = copies(0, p_in, 2, nx, 4, nv, unit)
    begin(made)
    flat = by_tap(w_first)
    for k in range(nv + 2):
        part = dot(flat, g_first[k]).astype(BF)
        for c in range(3):
            t_first[(c * (nv + 2) + k) * 16 : (c * (nv + 2) + k + 1) * 16] = part[c * 16 : c * 16 + 16]
    across = finish(0, made, p_in, q_in)
    for src, dst in ((w_enc, t_enc), (w_dec, t_dec)):
        flat = by_tap(src)
        for k in range(nv):
            part = dot(flat, g_fine[k]).astype(BF)
            for c in range(3):
                dst[(c * nv + k) * 16 : (c * nv + k + 1) * 16] = part[c * 16 : c * 16 + 16]
    across.wait()

    e2, e1 = edge(2), edge(1)
    fine_rows = (nv + 2) * 16
    row = lax.broadcasted_iota(jnp.int32, (fine_rows, 1), 0)
    v_low = jnp.where(iz > 0, 0, 16)
    v_high = jnp.where(iz < gz - 1, fine_rows, fine_rows - 16)
    v_ok = jnp.where((row >= v_low) & (row < v_high), 1.0, 0.0)
    both = jnp.concatenate([jnp.ones((1, ns), F32), e1.astype(F32)], axis=1)
    keep_first = v_ok * both

    def first_step(x, _):
        field = jnp.concatenate([rows(p_in, x, 3), rows(q_in, x, 3) * e2], axis=1)
        z = taps(dot(t_first[...], field), fine_rows)
        gone = ((x == 0) & (ix == 0)) | ((x == nx + 1) & (ix == gx - 1))
        first[x] = (silu(z) * keep_first * jnp.where(gone, 0.0, 1.0)).astype(BF)
        return 0

    lax.fori_loop(0, nx + 2, first_step, 0)

    def enc_step(x, _):
        z = taps(dot(t_enc[...], rows(first, x, 3)), nv * 16)[:, :ns]
        skip[x] = silu(z).astype(BF)
        return 0

    lax.fori_loop(0, nx, enc_step, 0)

    for k in range(mv):
        part = dot(w_down[...], g_down[k]).astype(BF)
        half = g_down.shape[2]
        for c in range(2):
            t_down[k * 64 : (k + 1) * 64, c * half : (c + 1) * half] = part[c * 64 : (c + 1) * 64]

    def down_step(x, _):
        y = dot(rows(skip, 2 * x, 2), l_down[...]).astype(BF)
        field = jnp.concatenate([y[:, :ns], y[:, ns:]], axis=0)
        p_mi[x + 1, 64 : (mv + 1) * 64] = silu(dot(t_down[...], field)).astype(BF)
        return 0

    lax.fori_loop(0, mx, down_step, 0)

    made = copies(1, p_mi, 1, mx, 1, mv, 64)
    begin(made)
    for k in range(mv):
        part = dot(w_ufine[...], g_up[k]).astype(BF)
        for a in range(2):
            t_up[a * nv * 16 + k * 32 : a * nv * 16 + k * 32 + 32] = part[a * 32 : a * 32 + 32]
    finish(1, made, p_mi, q_mi).wait()

    own_half = jnp.where(lane < ns // 2, 1.0, 0.0).astype(BF)
    mid_edge = jnp.where(lane == jnp.where(iy == 0, ns // 2, ns - 1), 1.0, 0.0).astype(BF)

    def mid_conv(w, p, q, x, v):
        pieces = []
        for a in range(3):
            r = pl.ds(pl.multiple_of(v * 64, 64), 192)
            pieces.append(p[x + a, r] * own_half + q[x + a, r] * mid_edge)
        z = silu(taps(dot(w[...], jnp.concatenate(pieces, axis=0)), 64))
        return jnp.where(lane < ns // 2, z, pltpu.roll(z, ns // 2, 1)).astype(BF)

    def menc_step(n, _):
        x, v = n // mv, n % mv
        mskip[x, pl.ds(pl.multiple_of(v * 64, 64), 64)] = mid_conv(w_menc, p_mi, q_mi, x, v)
        return 0

    lax.fori_loop(0, mx * mv, menc_step, 0)

    halves = []
    for a in range(2):
        total = None
        for n in range(bx * bv):
            x, v = n // bv, n % bv
            term = dot(mskip[2 * x + a, v * 128 : v * 128 + 128], l_bottom[n])
            total = term if total is None else total + term
        halves.append(total.astype(BF))
    field = jnp.concatenate(
        [halves[0][:, :ns], halves[1][:, :ns], halves[0][:, ns:], halves[1][:, ns:]], axis=0
    )
    bottom[...] = silu(dot(w_bot[...], field)).astype(BF)

    peers = []
    for d in range(1, gx):
        c = pltpu.make_async_remote_copy(
            src_ref=bottom, dst_ref=gathered.at[d - 1], send_sem=asend.at[d - 1], recv_sem=arecv.at[d - 1],
            device_id=(lax.rem(ix + d, gx), iy, iz), device_id_type=MESH,
        )
        c.start()
        peers.append(c)

    def normalize(block):
        f = block.astype(F32)
        return (f * lax.rsqrt(jnp.mean(f * f, axis=0, keepdims=True) + 1e-05)).astype(BF)

    chans = bottom.shape[0]
    depth = chans // HEADS
    own = normalize(bottom[...])
    queries = dot(w_q[...], own).astype(BF).astype(F32)
    scores, values = [], []
    for d in range(gx):
        if d:
            peers[d - 1].wait()
            normed = normalize(gathered[d - 1])
        else:
            normed = own
        keys = dot(w_k[...], normed).astype(BF).astype(F32)
        value = dot(w_v[...], normed).astype(BF).astype(F32)
        for turn in range(bx):
            k = pltpu.roll(keys, turn * (ns // bx), 1) if turn else keys
            v = pltpu.roll(value, turn * (ns // bx), 1) if turn else value
            scores.append(
                jnp.sum((queries * k).reshape(HEADS, depth, ns), axis=1, keepdims=True) * (depth**-0.5)
            )
            values.append(v)
    top = functools.reduce(jnp.maximum, scores)
    powers = [jnp.exp(s - top) for s in scores]
    norm = 1.0 / functools.reduce(jnp.add, powers)
    attended = None
    for s, v in zip(powers, values):
        term = (s * norm).astype(BF).astype(F32) * v.reshape(HEADS, depth, ns)
        attended = term if attended is None else attended + term
    attended = attended.reshape(chans, ns).astype(BF)
    mixed = (bottom[...].astype(F32) + dot(w_o[...], attended)).astype(BF)

    spread = dot(mixed, l_mid[...]).astype(BF)
    for n in range(bx * bv):
        x, v = n // bv, n % bv
        field = jnp.concatenate(
            [spread[:, 2 * n * ns : (2 * n + 1) * ns], spread[:, (2 * n + 1) * ns : (2 * n + 2) * ns]], axis=0
        )
        z = dot(w_umid[...], field)
        for a in range(2):
            old = mskip[2 * x + a, v * 128 : v * 128 + 128].astype(F32)
            p_mu[2 * x + a + 1, 64 + v * 128 : 64 + v * 128 + 128] = (z[a * 128 : a * 128 + 128] + old).astype(BF)

    made = copies(2, p_mu, 1, mx, 1, mv, 64)
    begin(made)
    finish(2, made, p_mu, q_mu).wait()

    def mdec_step(n, _):
        x, v = n // mv, n % mv
        mdec[x, pl.ds(pl.multiple_of(v * 64, 64), 64)] = mid_conv(w_mdec, p_mu, q_mu, x, v)
        return 0

    lax.fori_loop(0, mx * mv, mdec_step, 0)

    def up_step(x, _):
        y = dot(mdec[x], l_fine[...]).astype(BF)
        field = jnp.concatenate([y[:, :ns], y[:, ns:]], axis=0)
        z = dot(t_up[...], field)
        m = nv * 16
        for a in range(2):
            old = skip[2 * x + a].astype(F32)
            p_fu[2 * x + a + 1, 16 : 16 + m] = (z[a * m : (a + 1) * m] + old).astype(BF)
        return 0

    lax.fori_loop(0, mx, up_step, 0)

    made = copies(3, p_fu, 1, nx, 1, nv, 16)
    begin(made)
    finish(3, made, p_fu, q_fu).wait()

    def dec_step(x, _):
        field = jnp.concatenate([rows(p_fu, x, 3), rows(q_fu, x, 3) * e1], axis=1)
        z = taps(dot(t_dec[...], field), nv * 16)[:, :ns]
        wake = dot(w_hd[...], silu(z).astype(BF))
        for o in range(4):
            out[o, x] = wake[o * nv : (o + 1) * nv]
        return 0

    lax.fori_loop(0, nx, dec_step, 0)


def on_device(
    gx, gz, inputs, w_in, w_fine_enc, w_down_mid, w_mid_enc, w_down_bottom, w_query, w_key, w_value,
    w_attn_out, w_up_mid, w_mid_dec, w_up_fine, w_fine_dec, w_head,
):
    _, nx, nv, ns = inputs.shape
    mx, mv = nx // 2, nv // 2
    cells = (nx // 4) * (nv // 4) * (ns // 4)
    assert cells == ns and 2 * (nx // 4) == mx

    def taps_out(w):
        o, i = w.shape[:2]
        return w.transpose(4, 0, 2, 3, 1).reshape(w.shape[4] * o, -1)

    def each_tap(w):
        return w.transpose(2, 3, 4, 0, 1).reshape(27, w.shape[0], w.shape[1])

    def mid(w):
        return w.reshape(3, 3, 3, 64, 64).transpose(2, 3, 0, 1, 4).reshape(192, 576)

    local = inputs.transpose(1, 2, 0, 3).reshape(nx, nv * 4, ns)
    w_bot = w_down_bottom.reshape(2, 2, 2, 256, 64).transpose(3, 2, 0, 1, 4).reshape(256, 512)
    w_umid = w_up_mid.reshape(2, 2, 2, 256, 64).transpose(0, 1, 4, 2, 3).reshape(256, 512)
    w_ufine = w_up_fine.transpose(2, 3, 1, 4, 0).reshape(64, 128)
    w_hd = (w_head[:, None, None, :] * jnp.eye(nv, dtype=BF)[None, :, :, None]).reshape(4 * nv, nv * 16)
    operands = (
        local, each_tap(w_in), each_tap(w_fine_enc), taps_out(w_down_mid), mid(w_mid_enc), w_bot,
        w_query, w_key, w_value, w_attn_out, w_umid, mid(w_mid_dec), w_ufine, each_tap(w_fine_dec), w_hd,
    ) + constants(nx, nv, ns)
    vm = pltpu.VMEM
    shapes = []
    for shape in (
        (nx + 4, (nv + 8) * 4, ns), (mx + 2, (mv + 2) * 64, ns), (mx + 2, (mv + 2) * 64, ns),
        (nx + 2, (nv + 2) * 16, ns),
    ):
        shapes += [vm(shape, BF), vm(shape, BF)]
    return pl.pallas_call(
        functools.partial(kernel, gx, gz, nx, nv, ns),
        out_shape=jax.ShapeDtypeStruct(inputs.shape, F32),
        in_specs=[pl.BlockSpec(memory_space=pltpu.VMEM)] * len(operands),
        out_specs=pl.BlockSpec(memory_space=pltpu.VMEM),
        scratch_shapes=shapes + [
            vm((3 * (nv + 2) * 16, 3 * (nv + 8) * 4), BF),
            vm((3 * nv * 16, 3 * (nv + 2) * 16), BF),
            vm((3 * nv * 16, 3 * (nv + 2) * 16), BF),
            vm((mv * 64, 4 * nv * 16), BF),
            vm((2 * nv * 16, 2 * mv * 64), BF),
            vm((nx + 2, (nv + 2) * 16, 2 * ns), BF),
            vm((nx, nv * 16, ns), BF),
            vm((mx, mv * 64, ns), BF),
            vm((mx, mv * 64, ns), BF),
            vm((256, cells), BF),
            vm((max(gx - 1, 1), 256, cells), BF),
            pltpu.SemaphoreType.DMA((4, 8)),
            pltpu.SemaphoreType.DMA((4, 8)),
            pltpu.SemaphoreType.DMA((4,)),
            pltpu.SemaphoreType.DMA((4,)),
            pltpu.SemaphoreType.DMA((max(gx - 1, 1),)),
            pltpu.SemaphoreType.DMA((max(gx - 1, 1),)),
        ],
        compiler_params=pltpu.CompilerParams(
            collective_id=0, has_side_effects=True, vmem_limit_bytes=48 * 1024 * 1024
        ),
    )(*operands)


def solution(mesh):
    cells = P(None, "gx", "gz", "gy")
    return jax.shard_map(
        functools.partial(on_device, mesh.shape["gx"], mesh.shape["gz"]),
        mesh=mesh, in_specs=(cells,) + (P(),) * 14, out_specs=cells, check_vma=False,
    )
```

```python
import functools

import jax
import jax.numpy as jnp
import numpy as np
from jax import lax
from jax.experimental import pallas as pl
from jax.experimental.pallas import tpu as pltpu
from jax.sharding import PartitionSpec as P

BF = jnp.bfloat16
F32 = jnp.float32
MESH = pl.DeviceIdType.MESH
HEADS = 4
FAR = 17
DIRS = tuple((dx, dv) for dx in (-1, 0, 1) for dv in (-1, 0, 1) if (dx, dv) != (0, 0))


def constants(nx, nv, ns):
    mv, ms, bv, bs = nv // 2, ns // 2, nv // 4, ns // 4
    g_first = np.zeros((nv + 2, 3, 3, 4, 3, nv + 8, 4), np.float32)
    for k in range(nv + 2):
        for a in range(3):
            for b in range(3):
                for i in range(4):
                    g_first[k, a, b, i, a, k + b + 2, i] = 1
    g_fine = np.zeros((nv, 3, 3, 16, 3, nv + 2, 16), np.float32)
    for k in range(nv):
        for a in range(3):
            for b in range(3):
                for i in range(16):
                    g_fine[k, a, b, i, a, k + b, i] = 1
    g_down = np.zeros((mv, 2, 2, 16, 2, nv, 16), np.float32)
    for k in range(mv):
        for a in range(2):
            for b in range(2):
                for i in range(16):
                    g_down[k, a, b, i, a, 2 * k + b, i] = 1
    g_up = np.zeros((mv, 2, 64, 2, mv, 64), np.float32)
    for k in range(mv):
        for c in range(2):
            for i in range(64):
                g_up[k, c, i, c, k, i] = 1
    lane_down = np.zeros((ns, 2, 2, ms), np.float32)
    for c in range(2):
        for t in range(ms):
            lane_down[2 * t + c, c, :, t] = 1
    cells = 2 * bv * bs
    lane_bottom = np.zeros((2 * bv, ns, 2, 2 * bv, bs), np.float32)
    for q in range(2 * bv):
        for c in range(2):
            for t in range(bs):
                lane_bottom[q, 2 * t + c, c, q, t] = 1
    lane_mid = np.zeros((2 * bv, bs, 2 * bv, 2, 2, ms), np.float32)
    for q in range(2 * bv):
        for c in range(2):
            for t in range(bs):
                lane_mid[q, t, q, c, :, 2 * t + c] = 1
    lane_fine = np.zeros((ns, 2, ns), np.float32)
    for c in range(2):
        for u in range(ms):
            lane_fine[u, c, 2 * u + c] = 1
    arrays = (
        g_first.reshape(nv + 2, 36, 3 * (nv + 8) * 4),
        g_fine.reshape(nv, 144, 3 * (nv + 2) * 16),
        g_down.reshape(mv, 64, 2 * nv * 16),
        g_up.reshape(mv, 128, 2 * mv * 64),
        lane_down.reshape(ns, 2 * ns),
        lane_bottom.reshape(2 * bv, ns, 2 * cells),
        lane_mid.reshape(cells, 2 * bv * 2 * ns),
        lane_fine.reshape(ns, 2 * ns),
    )
    return tuple(jnp.asarray(np.asarray(a, jnp.bfloat16)) for a in arrays)


def dot(a, b):
    return jnp.dot(a, b, preferred_element_type=F32)


def silu(x):
    h = 0.5 * x
    return h + h * jnp.tanh(h)


def rows(ref, x, n):
    part = ref[pl.ds(x, n)]
    return part.reshape(n * part.shape[1], part.shape[2])


def by_tap(ref):
    parts = []
    for c in range(3):
        parts.append(jnp.concatenate([ref[ab * 3 + c].astype(F32) for ab in range(9)], axis=1))
    return jnp.concatenate(parts, axis=0).astype(BF)


def taps(z, m):
    n = z.shape[1]
    return pltpu.roll(z[0:m], 1, 1) + z[m : 2 * m] + pltpu.roll(z[2 * m : 3 * m], n - 1, 1)


def kernel(
    gx, gz, nx, nv, ns,
    inp, w_first, w_enc, w_down, g_first, w_dec, *rest
):
    far, rest = rest[:FAR], rest[FAR:]
    (
        out,
        p_in, q_in, p_mi, q_mi, p_mu, q_mu, p_fu, q_fu,
        t_first, t_enc, t_dec, t_down, t_up, first, skip, mskip, mdec, bottom, gathered,
        send, recv, csend, crecv, asend, arecv, fsem,
    ), near = rest[:-FAR], rest[-FAR:]
    fetches = []
    for n in range(FAR):
        c = pltpu.make_async_copy(far[n], near[n], fsem.at[n])
        c.start()
        fetches.append(c)
    (
        g_fine, g_down, g_up, l_down, l_bottom, l_mid, l_fine,
        w_menc, w_bot, w_q, w_k, w_v, w_o, w_umid, w_mdec, w_ufine, w_hd,
    ) = near
    mx, mv = nx // 2, nv // 2
    bx, bv = nx // 4, nv // 4
    ix, iy, iz = lax.axis_index("gx"), lax.axis_index("gy"), lax.axis_index("gz")

    def inside(dx, dv):
        ok = None
        for d, i, n in ((dx, ix, gx), (dv, iz, gz)):
            if d:
                here = (i + d >= 0) & (i + d < n)
                ok = here if ok is None else ok & here
        return ok

    def target(dx, dv):
        return (ix + dx, iy, iz + dv)

    for ref in (p_in, p_mi, p_mu, p_fu):
        ref[...] = jnp.zeros_like(ref)

    barrier = pltpu.get_barrier_semaphore()
    pl.semaphore_signal(barrier, inc=1, device_id=(ix, 1 - iy, iz), device_id_type=MESH)
    for d in range(1, gx):
        pl.semaphore_signal(
            barrier, inc=1, device_id=(lax.rem(ix + d, gx), iy, iz), device_id_type=MESH
        )
    count = gx
    for dx, dv in DIRS:
        if dv:
            ok = inside(dx, dv)

            @pl.when(ok)
            def _(dx=dx, dv=dv):
                pl.semaphore_signal(barrier, inc=1, device_id=target(dx, dv), device_id_type=MESH)

            count = count + ok.astype(jnp.int32)
    pl.semaphore_wait(barrier, count)

    def span(d, width, size, unit):
        if d > 0:
            return pl.ds(size * unit, width * unit), pl.ds(0, width * unit)
        if d < 0:
            return pl.ds(width * unit, width * unit), pl.ds((width + size) * unit, width * unit)
        return pl.ds(width * unit, size * unit), pl.ds(width * unit, size * unit)

    def copies(e, p, wx, sx, wv, sv, unit):
        made = []
        for n, (dx, dv) in enumerate(DIRS):
            src_x, dst_x = span(dx, wx, sx, 1)
            src_v, dst_v = span(dv, wv, sv, unit)
            made.append(
                pltpu.make_async_remote_copy(
                    src_ref=p.at[src_x, src_v],
                    dst_ref=p.at[dst_x, dst_v],
                    send_sem=send.at[e, n],
                    recv_sem=recv.at[e, n],
                    device_id=target(dx, dv),
                    device_id_type=MESH,
                )
            )
        return made

    def begin(made):
        for c, (dx, dv) in zip(made, DIRS):
            pl.when(inside(dx, dv))(c.start)

    def finish(e, made, p, q):
        for c, (dx, dv) in zip(made, DIRS):
            pl.when(inside(-dx, -dv))(c.wait_recv)
        across = pltpu.make_async_remote_copy(
            src_ref=p, dst_ref=q, send_sem=csend.at[e], recv_sem=crecv.at[e],
            device_id=(ix, 1 - iy, iz), device_id_type=MESH,
        )
        across.start()
        for c, (dx, dv) in zip(made, DIRS):
            pl.when(inside(dx, dv))(c.wait_send)
        return across

    lane = lax.broadcasted_iota(jnp.int32, (1, ns), 1)

    def edge(width):
        low = jnp.where(iy == 0, 0, ns - width)
        return jnp.where((lane >= low) & (lane < low + width), 1.0, 0.0).astype(BF)

    unit = inp.shape[1] // nv
    p_in[2 : 2 + nx, 4 * unit : (4 + nv) * unit] = inp[...]
    made = copies(0, p_in, 2, nx, 4, nv, unit)
    begin(made)
    flat = by_tap(w_first)
    for k in range(nv + 2):
        part = dot(flat, g_first[k]).astype(BF)
        for c in range(3):
            t_first[(c * (nv + 2) + k) * 16 : (c * (nv + 2) + k + 1) * 16] = part[c * 16 : c * 16 + 16]
    across = finish(0, made, p_in, q_in)
    for c in fetches:
        c.wait()
    for src, dst in ((w_enc, t_enc), (w_dec, t_dec)):
        flat = by_tap(src)
        for k in range(nv):
            part = dot(flat, g_fine[k]).astype(BF)
            for c in range(3):
                dst[(c * nv + k) * 16 : (c * nv + k + 1) * 16] = part[c * 16 : c * 16 + 16]
    across.wait()

    e2, e1 = edge(2), edge(1)
    fine_rows = (nv + 2) * 16
    row = lax.broadcasted_iota(jnp.int32, (fine_rows, 1), 0)
    v_low = jnp.where(iz > 0, 0, 16)
    v_high = jnp.where(iz < gz - 1, fine_rows, fine_rows - 16)
    v_ok = jnp.where((row >= v_low) & (row < v_high), 1.0, 0.0)
    both = jnp.concatenate([jnp.ones((1, ns), F32), e1.astype(F32)], axis=1)
    keep_first = v_ok * both

    def first_step(x, _):
        field = jnp.concatenate([rows(p_in, x, 3), rows(q_in, x, 3) * e2], axis=1)
        z = taps(dot(t_first[...], field), fine_rows)
        gone = ((x == 0) & (ix == 0)) | ((x == nx + 1) & (ix == gx - 1))
        first[x] = (silu(z) * keep_first * jnp.where(gone, 0.0, 1.0)).astype(BF)
        return 0

    lax.fori_loop(0, nx + 2, first_step, 0)

    def enc_step(x, _):
        z = taps(dot(t_enc[...], rows(first, x, 3)), nv * 16)[:, :ns]
        skip[x] = silu(z).astype(BF)
        return 0

    lax.fori_loop(0, nx, enc_step, 0)

    for k in range(mv):
        part = dot(w_down[...], g_down[k]).astype(BF)
        half = g_down.shape[2]
        for c in range(2):
            t_down[k * 64 : (k + 1) * 64, c * half : (c + 1) * half] = part[c * 64 : (c + 1) * 64]

    def down_step(x, _):
        y = dot(rows(skip, 2 * x, 2), l_down[...]).astype(BF)
        field = jnp.concatenate([y[:, :ns], y[:, ns:]], axis=0)
        p_mi[x + 1, 64 : (mv + 1) * 64] = silu(dot(t_down[...], field)).astype(BF)
        return 0

    lax.fori_loop(0, mx, down_step, 0)

    made = copies(1, p_mi, 1, mx, 1, mv, 64)
    begin(made)
    for k in range(mv):
        part = dot(w_ufine[...], g_up[k]).astype(BF)
        for a in range(2):
            t_up[a * nv * 16 + k * 32 : a * nv * 16 + k * 32 + 32] = part[a * 32 : a * 32 + 32]
    finish(1, made, p_mi, q_mi).wait()

    own_half = jnp.where(lane < ns // 2, 1.0, 0.0).astype(BF)
    mid_edge = jnp.where(lane == jnp.where(iy == 0, ns // 2, ns - 1), 1.0, 0.0).astype(BF)

    def mid_conv(w, p, q, x, v):
        pieces = []
        for a in range(3):
            r = pl.ds(pl.multiple_of(v * 64, 64), 192)
            pieces.append(p[x + a, r] * own_half + q[x + a, r] * mid_edge)
        z = silu(taps(dot(w[...], jnp.concatenate(pieces, axis=0)), 64))
        return jnp.where(lane < ns // 2, z, pltpu.roll(z, ns // 2, 1)).astype(BF)

    def menc_step(n, _):
        x, v = n // mv, n % mv
        mskip[x, pl.ds(pl.multiple_of(v * 64, 64), 64)] = mid_conv(w_menc, p_mi, q_mi, x, v)
        return 0

    lax.fori_loop(0, mx * mv, menc_step, 0)

    halves = []
    for a in range(2):
        total = None
        for n in range(bx * bv):
            x, v = n // bv, n % bv
            term = dot(mskip[2 * x + a, v * 128 : v * 128 + 128], l_bottom[n])
            total = term if total is None else total + term
        halves.append(total.astype(BF))
    field = jnp.concatenate(
        [halves[0][:, :ns], halves[1][:, :ns], halves[0][:, ns:], halves[1][:, ns:]], axis=0
    )
    bottom[...] = silu(dot(w_bot[...], field)).astype(BF)

    peers = []
    for d in range(1, gx):
        c = pltpu.make_async_remote_copy(
            src_ref=bottom, dst_ref=gathered.at[d - 1], send_sem=asend.at[d - 1], recv_sem=arecv.at[d - 1],
            device_id=(lax.rem(ix + d, gx), iy, iz), device_id_type=MESH,
        )
        c.start()
        peers.append(c)

    def normalize(block):
        f = block.astype(F32)
        return (f * lax.rsqrt(jnp.mean(f * f, axis=0, keepdims=True) + 1e-05)).astype(BF)

    chans = bottom.shape[0]
    depth = chans // HEADS
    own = normalize(bottom[...])
    queries = dot(w_q[...], own).astype(BF).astype(F32)
    scores, values = [], []
    for d in range(gx):
        if d:
            peers[d - 1].wait()
            normed = normalize(gathered[d - 1])
        else:
            normed = own
        keys = dot(w_k[...], normed).astype(BF).astype(F32)
        value = dot(w_v[...], normed).astype(BF).astype(F32)
        for turn in range(bx):
            k = pltpu.roll(keys, turn * (ns // bx), 1) if turn else keys
            v = pltpu.roll(value, turn * (ns // bx), 1) if turn else value
            scores.append(
                jnp.sum((queries * k).reshape(HEADS, depth, ns), axis=1, keepdims=True) * (depth**-0.5)
            )
            values.append(v)
    top = functools.reduce(jnp.maximum, scores)
    powers = [jnp.exp(s - top) for s in scores]
    norm = 1.0 / functools.reduce(jnp.add, powers)
    attended = None
    for s, v in zip(powers, values):
        term = (s * norm).astype(BF).astype(F32) * v.reshape(HEADS, depth, ns)
        attended = term if attended is None else attended + term
    attended = attended.reshape(chans, ns).astype(BF)
    mixed = (bottom[...].astype(F32) + dot(w_o[...], attended)).astype(BF)

    spread = dot(mixed, l_mid[...]).astype(BF)
    for n in range(bx * bv):
        x, v = n // bv, n % bv
        field = jnp.concatenate(
            [spread[:, 2 * n * ns : (2 * n + 1) * ns], spread[:, (2 * n + 1) * ns : (2 * n + 2) * ns]], axis=0
        )
        z = dot(w_umid[...], field)
        for a in range(2):
            old = mskip[2 * x + a, v * 128 : v * 128 + 128].astype(F32)
            p_mu[2 * x + a + 1, 64 + v * 128 : 64 + v * 128 + 128] = (z[a * 128 : a * 128 + 128] + old).astype(BF)

    made = copies(2, p_mu, 1, mx, 1, mv, 64)
    begin(made)
    finish(2, made, p_mu, q_mu).wait()

    def mdec_step(n, _):
        x, v = n // mv, n % mv
        mdec[x, pl.ds(pl.multiple_of(v * 64, 64), 64)] = mid_conv(w_mdec, p_mu, q_mu, x, v)
        return 0

    lax.fori_loop(0, mx * mv, mdec_step, 0)

    def up_step(x, _):
        y = dot(mdec[x], l_fine[...]).astype(BF)
        field = jnp.concatenate([y[:, :ns], y[:, ns:]], axis=0)
        z = dot(t_up[...], field)
        m = nv * 16
        for a in range(2):
            old = skip[2 * x + a].astype(F32)
            p_fu[2 * x + a + 1, 16 : 16 + m] = (z[a * m : (a + 1) * m] + old).astype(BF)
        return 0

    lax.fori_loop(0, mx, up_step, 0)

    made = copies(3, p_fu, 1, nx, 1, nv, 16)
    begin(made)
    finish(3, made, p_fu, q_fu).wait()

    def dec_step(x, _):
        field = jnp.concatenate([rows(p_fu, x, 3), rows(q_fu, x, 3) * e1], axis=1)
        z = taps(dot(t_dec[...], field), nv * 16)[:, :ns]
        wake = dot(w_hd[...], silu(z).astype(BF))
        for o in range(4):
            out[o, x] = wake[o * nv : (o + 1) * nv]
        return 0

    lax.fori_loop(0, nx, dec_step, 0)


def on_device(
    gx, gz, inputs, w_in, w_fine_enc, w_down_mid, w_mid_enc, w_down_bottom, w_query, w_key, w_value,
    w_attn_out, w_up_mid, w_mid_dec, w_up_fine, w_fine_dec, w_head,
):
    _, nx, nv, ns = inputs.shape
    mx, mv = nx // 2, nv // 2
    cells = (nx // 4) * (nv // 4) * (ns // 4)
    assert cells == ns and 2 * (nx // 4) == mx

    def taps_out(w):
        o, i = w.shape[:2]
        return w.transpose(4, 0, 2, 3, 1).reshape(w.shape[4] * o, -1)

    def each_tap(w):
        return w.transpose(2, 3, 4, 0, 1).reshape(27, w.shape[0], w.shape[1])

    def mid(w):
        return w.reshape(3, 3, 3, 64, 64).transpose(2, 3, 0, 1, 4).reshape(192, 576)

    local = inputs.transpose(1, 2, 0, 3).reshape(nx, nv * 4, ns)
    w_bot = w_down_bottom.reshape(2, 2, 2, 256, 64).transpose(3, 2, 0, 1, 4).reshape(256, 512)
    w_umid = w_up_mid.reshape(2, 2, 2, 256, 64).transpose(0, 1, 4, 2, 3).reshape(256, 512)
    w_ufine = w_up_fine.transpose(2, 3, 1, 4, 0).reshape(64, 128)
    w_hd = (w_head[:, None, None, :] * jnp.eye(nv, dtype=BF)[None, :, :, None]).reshape(4 * nv, nv * 16)
    g_first, *fixed = constants(nx, nv, ns)
    far = (
        *fixed, mid(w_mid_enc), w_bot, w_query, w_key, w_value, w_attn_out, w_umid, mid(w_mid_dec), w_ufine, w_hd,
    )
    assert len(far) == FAR
    operands = (
        local, each_tap(w_in), each_tap(w_fine_enc), taps_out(w_down_mid), g_first, each_tap(w_fine_dec),
    )
    vm = pltpu.VMEM
    shapes = []
    for shape in (
        (nx + 4, (nv + 8) * 4, ns), (mx + 2, (mv + 2) * 64, ns), (mx + 2, (mv + 2) * 64, ns),
        (nx + 2, (nv + 2) * 16, ns),
    ):
        shapes += [vm(shape, BF), vm(shape, BF)]
    return pl.pallas_call(
        functools.partial(kernel, gx, gz, nx, nv, ns),
        out_shape=jax.ShapeDtypeStruct(inputs.shape, F32),
        in_specs=[pl.BlockSpec(memory_space=pltpu.VMEM)] * len(operands)
        + [pl.BlockSpec(memory_space=pl.ANY)] * FAR,
        out_specs=pl.BlockSpec(memory_space=pltpu.VMEM),
        scratch_shapes=shapes + [
            vm((3 * (nv + 2) * 16, 3 * (nv + 8) * 4), BF),
            vm((3 * nv * 16, 3 * (nv + 2) * 16), BF),
            vm((3 * nv * 16, 3 * (nv + 2) * 16), BF),
            vm((mv * 64, 4 * nv * 16), BF),
            vm((2 * nv * 16, 2 * mv * 64), BF),
            vm((nx + 2, (nv + 2) * 16, 2 * ns), BF),
            vm((nx, nv * 16, ns), BF),
            vm((mx, mv * 64, ns), BF),
            vm((mx, mv * 64, ns), BF),
            vm((256, cells), BF),
            vm((max(gx - 1, 1), 256, cells), BF),
            pltpu.SemaphoreType.DMA((4, 8)),
            pltpu.SemaphoreType.DMA((4, 8)),
            pltpu.SemaphoreType.DMA((4,)),
            pltpu.SemaphoreType.DMA((4,)),
            pltpu.SemaphoreType.DMA((max(gx - 1, 1),)),
            pltpu.SemaphoreType.DMA((max(gx - 1, 1),)),
            pltpu.SemaphoreType.DMA((FAR,)),
        ] + [vm(a.shape, BF) for a in far],
        compiler_params=pltpu.CompilerParams(
            collective_id=0, has_side_effects=True, vmem_limit_bytes=48 * 1024 * 1024
        ),
    )(*operands, *far)


def solution(mesh):
    cells = P(None, "gx", "gz", "gy")
    return jax.shard_map(
        functools.partial(on_device, mesh.shape["gx"], mesh.shape["gz"]),
        mesh=mesh, in_specs=(cells,) + (P(),) * 14, out_specs=cells, check_vma=False,
    )
```
